32 devices in a mesh: dp: 4 (over y, x), tensor: 8 (over z, core).
Axes of the slice: x: 2, y: 2, z: 4, core: 2. Of those that a mesh axis runs over, the one named last changes fastest.
Arguments:
- tokens: bfloat16 [512, 8192], P('tensor', 'dp'), may hold values from -6 to 6
- cotangent: bfloat16 [512, 8192], P('tensor', 'dp'), may hold values from -0.625 to 0.625
- gate_weight: bfloat16 [8192, 14336], P('dp', 'tensor'), may hold values from -0.0625 to 0.0625
- up_weight: bfloat16 [8192, 14336], P('dp', 'tensor'), may hold values from -0.0625 to 0.0625
- down_weight: bfloat16 [14336, 8192], P('tensor', 'dp'), may hold values from -0.046875 to 0.046875
- gate_in: bfloat16 [16, 8192, 16], P(None, 'dp'), may hold values from -0.0625 to 0.0625
- up_in: bfloat16 [16, 8192, 16], P(None, 'dp'), may hold values from -0.0625 to 0.0625
- down_out: bfloat16 [16, 16, 8192], P(None, None, 'dp'), may hold values from -1.5 to 1.5
- gate_out: bfloat16 [16, 16, 14336], P(None, None, 'tensor'), may hold values from -1.5 to 1.5
- up_out: bfloat16 [16, 16, 14336], P(None, None, 'tensor'), may hold values from -1.5 to 1.5
- down_in: bfloat16 [16, 14336, 16], P(None, 'tensor'), may hold values from -0.046875 to 0.046875
- tenants: int32 [8], replicated, may hold values from 0 to 15
- owners: int32 [16], replicated, may hold values from 0 to 15, each once
Outputs:
- mixed: bfloat16 [512, 8192], P('tensor', 'dp')
- grad_gate_in: float32 [16, 8192, 16], P('tensor', 'dp')
- grad_up_in: float32 [16, 8192, 16], P('tensor', 'dp')
- grad_down_out: float32 [16, 16, 8192], P('tensor', None, 'dp')
- grad_gate_out: float32 [16, 16, 14336], P('dp', None, 'tensor')
- grad_up_out: float32 [16, 16, 14336], P('dp', None, 'tensor')
- grad_down_in: float32 [16, 14336, 16], P('dp', 'tensor')
The draws below stay inside these ranges and needn't reach their ends.
Inputs may be any that keep to these rules, and one draw needn't show every extreme that they name: `tenants`: tenant numbers lie in 0 to 15; a tenant may own no block. `owners`: every owner slot is given to exactly one tenant.
All inputs are finite; a program needn't handle non-finite values.
Results may differ from the reference program's by a relative error of at most 0.029.
Values may be sent and summed in bfloat16 or wider, within the bound.
A program may use at most 128 MiB of HBM per device.

```python
import math
import jax
import jax.numpy as jnp
import numpy as np
from jax import lax

MODEL_WIDTH = 8192
FFW = 14336
R = 16
BLOCK = 64
TENANTS = 16
TOKENS = 512
NBLK = 8
N_DP = 4
N_TENSOR = 8


def set_ends(result, own_key, least, high):
    extent = result.shape
    place = [jax.random.randint(jax.random.fold_in(own_key, axis), (), 0, extent[axis]) for axis in range(len(extent))]
    result = result.at[tuple(place)].set(least)
    longest = extent.index(max(extent))
    place[longest] = (place[longest] + 1) % extent[longest]
    return result.at[tuple(place)].set(high)


def block_levels(own_key, shape, cuts, smallest, high):
    level = 1.0
    for axis_at, shards_of in cuts:
        draws = jax.random.uniform(jax.random.fold_in(jax.random.fold_in(own_key, 6), axis_at), (shards_of,), jnp.float32, smallest / len(cuts), high / len(cuts))
        level = level * jnp.repeat(jnp.exp(draws), shape[axis_at] // shards_of).reshape((-1,) + (1,) * (len(shape) - 1 - axis_at))
    return level


def rank_bounds(amount, slope):
    portions = [(1 << 20) // math.isqrt(rank ** slope) + 1 for rank in range(1, amount + 1)]
    scale = 1 + sum(portions) // (1 << 30)
    return np.cumsum(np.array([max(1, weight // scale) for weight in portions]))


def ranked(stream_key, dims, number_of, lean):
    listing = rank_bounds(number_of, lean)
    lot = jax.random.randint(jax.random.fold_in(stream_key, 1), dims, 0, int(listing[number_of - 1]))
    grade = jnp.searchsorted(jnp.asarray(listing, jnp.int32), lot, side="right")
    return jax.random.permutation(jax.random.fold_in(stream_key, 2), number_of)[grade].astype(jnp.int32)


def normal_values(stream_key, extent, scale, bound, cuts=(), held_as=jnp.bfloat16):
    drawn = jax.random.normal(stream_key, extent, jnp.float32) * scale
    if len(cuts) > 0:
        drawn = block_levels(stream_key, extent, cuts, -0.22, 0.18) * drawn
    return jnp.clip(drawn, min=-bound, max=bound).astype(held_as)


def setup_inputs(seed: int = 0) -> dict:
    splits = jax.random.split(jax.random.key(seed), 14)
    return {
        "tokens": normal_values(splits[0], (TOKENS, MODEL_WIDTH), 1.0, 6.0, ((0, 8), (1, 4))),
        "cotangent": normal_values(splits[1], (TOKENS, MODEL_WIDTH), 0.04, 0.625, ((0, 8), (1, 4))),
        "gate_weight": normal_values(splits[2], (MODEL_WIDTH, FFW), MODEL_WIDTH ** -0.5, 0.0625, ((0, 4), (1, 8))),
        "up_weight": normal_values(splits[3], (MODEL_WIDTH, FFW), MODEL_WIDTH ** -0.5, 0.0625, ((0, 4), (1, 8))),
        "down_weight": normal_values(splits[4], (FFW, MODEL_WIDTH), FFW ** -0.5, 0.046875, ((0, 8), (1, 4))),
        "gate_in": normal_values(splits[5], (TENANTS, MODEL_WIDTH, R), MODEL_WIDTH ** -0.5, 0.0625, ((1, 4),)),
        "up_in": normal_values(splits[6], (TENANTS, MODEL_WIDTH, R), MODEL_WIDTH ** -0.5, 0.0625, ((1, 4),)),
        "down_out": normal_values(splits[7], (TENANTS, R, MODEL_WIDTH), R ** -0.5, 1.5, ((2, 4),)),
        "gate_out": normal_values(splits[8], (TENANTS, R, FFW), R ** -0.5, 1.5, ((2, 8),)),
        "up_out": normal_values(splits[9], (TENANTS, R, FFW), R ** -0.5, 1.5, ((2, 8),)),
        "down_in": normal_values(splits[10], (TENANTS, FFW, R), FFW ** -0.5, 0.046875, ((1, 8),)),
        "tenants": set_ends(ranked(splits[11], (NBLK,), TENANTS, 2), jax.random.fold_in(splits[11], 3), 0, TENANTS - 1).astype(jnp.int32),
        "owners": jax.random.permutation(splits[12], TENANTS).astype(jnp.int32),
    }


adapter_scale = 0.5


def split_product(left, right, pieces):
    width = left.shape[1] // pieces
    total = jnp.zeros((left.shape[0], right.shape[1]), jnp.float32)
    for piece in range(pieces):
        term = jnp.dot(left[:, piece * width:(piece + 1) * width], right[piece * width:(piece + 1) * width], preferred_element_type=jnp.float32)
        term = lax.optimization_barrier(term.astype(jnp.bfloat16))
        total = total + term.astype(jnp.float32)
    return total


def split_product_back(left, right, pieces):
    width = left.shape[1] // pieces
    total = jnp.zeros((left.shape[0], right.shape[0]), jnp.float32)
    for piece in range(pieces):
        term = lax.dot_general(left[:, piece * width:(piece + 1) * width], right[:, piece * width:(piece + 1) * width], (((1,), (1,)), ((), ())), preferred_element_type=jnp.float32)
        term = lax.optimization_barrier(term.astype(jnp.bfloat16))
        total = total + term.astype(jnp.float32)
    return total


def split_rank(left_blocks, chosen, pieces):
    width = left_blocks.shape[2] // pieces
    total = jnp.zeros((left_blocks.shape[0], left_blocks.shape[1], chosen.shape[2]), jnp.float32)
    for piece in range(pieces):
        term = jnp.einsum("btk,bkr->btr", left_blocks[:, :, piece * width:(piece + 1) * width].astype(jnp.float32), chosen[:, piece * width:(piece + 1) * width].astype(jnp.float32))
        term = lax.optimization_barrier(term.astype(jnp.bfloat16))
        total = total + term.astype(jnp.float32)
    return total


def reference(tokens, cotangent, gate_weight, up_weight, down_weight, gate_in, up_in, down_out, gate_out, up_out, down_in, tenants, owners):
    highest = lax.Precision.HIGHEST
    blocks_all = tenants.shape[0]
    every_token_row = tokens.shape[0]
    input_blocks = tokens.reshape(blocks_all, BLOCK, MODEL_WIDTH)
    gate_frozen_term = split_product(tokens, gate_weight, N_DP).reshape(blocks_all, BLOCK, FFW)
    up_frozen_term = split_product(tokens, up_weight, N_DP).reshape(blocks_all, BLOCK, FFW)
    gate_rank_second = split_rank(input_blocks, gate_in[tenants], N_DP).astype(jnp.bfloat16).astype(jnp.float32)
    up_rank_second = split_rank(input_blocks, up_in[tenants], N_DP).astype(jnp.bfloat16).astype(jnp.float32)
    gate_raise = gate_out[tenants].astype(jnp.float32)
    up_raise = up_out[tenants].astype(jnp.float32)
    gate_complete = gate_frozen_term + adapter_scale * jnp.einsum("uim,umn->uin", gate_rank_second, gate_raise)
    up_complete = up_frozen_term + adapter_scale * jnp.einsum("uim,umn->uin", up_rank_second, up_raise)
    hidden = (jax.nn.silu(gate_complete) * up_complete).astype(jnp.bfloat16)
    output_frozen_term = split_product(hidden.reshape(every_token_row, FFW), down_weight, N_TENSOR).reshape(blocks_all, BLOCK, MODEL_WIDTH)
    down_rank_second = split_rank(hidden, down_in[tenants], N_TENSOR).astype(jnp.bfloat16).astype(jnp.float32)
    down_raise = down_out[tenants].astype(jnp.float32)
    mixed = (output_frozen_term + adapter_scale * jnp.einsum("vmn,vnx->vmx", down_rank_second, down_raise)).astype(jnp.bfloat16).reshape(every_token_row, MODEL_WIDTH)

    cotangent_block_list = cotangent.reshape(blocks_all, BLOCK, MODEL_WIDTH).astype(jnp.float32)
    down_backward = (adapter_scale * jnp.einsum("env,ejv->enj", cotangent_block_list, down_raise)).astype(jnp.bfloat16).astype(jnp.float32)
    tenant_ids = jnp.arange(TENANTS, dtype=jnp.int32)
    tenant_onehot = (tenant_ids[:, None] == tenants[None, :]).astype(jnp.float32)
    slot_onehot = (tenant_ids[:, None] == owners[tenants][None, :]).astype(jnp.float32)
    raise_block_list = adapter_scale * jnp.einsum("jpy,jpz->jyz", down_rank_second, cotangent_block_list)
    grad_down_out = jnp.einsum("eb,brd->erd", tenant_onehot, raise_block_list, precision=highest)
    hidden_grad = split_product_back(cotangent, down_weight, N_DP).reshape(blocks_all, BLOCK, FFW)
    hidden_grad = hidden_grad + jnp.einsum("btr,bfr->btf", down_backward, down_in[tenants].astype(jnp.float32))
    sig = jax.nn.sigmoid(gate_complete)
    up_gradient = (hidden_grad * gate_complete * sig).astype(jnp.bfloat16).astype(jnp.float32)
    gate_gradient = (hidden_grad * up_complete * sig * (1.0 + gate_complete * (1.0 - sig))).astype(jnp.bfloat16).astype(jnp.float32)
    gate_backward = (adapter_scale * jnp.einsum("yae,yve->yav", gate_gradient, gate_raise)).astype(jnp.bfloat16).astype(jnp.float32)
    up_backward = (adapter_scale * jnp.einsum("yae,yve->yav", up_gradient, up_raise)).astype(jnp.bfloat16).astype(jnp.float32)
    input_float = input_blocks.astype(jnp.float32)
    grad_gate_in = jnp.einsum("eb,bdr->edr", tenant_onehot, jnp.einsum("btd,btr->bdr", input_float, gate_backward), precision=highest)
    grad_up_in = jnp.einsum("eb,bdr->edr", tenant_onehot, jnp.einsum("btd,btr->bdr", input_float, up_backward), precision=highest)
    gate_raise_block_list = adapter_scale * jnp.einsum("yap,yau->ypu", gate_rank_second, gate_gradient)
    up_raise_block_list = adapter_scale * jnp.einsum("yap,yau->ypu", up_rank_second, up_gradient)
    grad_gate_out = jnp.einsum("sb,brf->srf", slot_onehot, gate_raise_block_list, precision=highest)
    grad_up_out = jnp.einsum("sb,brf->srf", slot_onehot, up_raise_block_list, precision=highest)
    drop_blocks = jnp.einsum("btf,btr->bfr", hidden.astype(jnp.float32), down_backward)
    grad_down_in = jnp.einsum("sb,bfr->sfr", slot_onehot, drop_blocks, precision=highest)
    return (mixed, grad_gate_in, grad_up_in, grad_down_out, grad_gate_out, grad_up_out, grad_down_in)
```

```python
import jax
import jax.numpy as jnp
from jax import lax
from jax.sharding import PartitionSpec as P

BLOCK = 64


adapter_scale = 0.5


def dot(a, b, ca=1, cb=0, precision=None):
    return lax.dot_general(
        a,
        b,
        (((ca,), (cb,)), ((), ())),
        preferred_element_type=jnp.float32,
        precision=precision,
    )


def flip(x, axis, bits):
    n = lax.axis_size(axis)
    return lax.ppermute(x, axis, [(i, i ^ bits) for i in range(n)])


def rows(x, index, count):
    return lax.dynamic_slice_in_dim(x, index * count, count)


def put(whole, x, index):
    return lax.dynamic_update_slice_in_dim(whole, x, index * x.shape[0], 0)


def gather_far(x, axis, step):
    return {b: x if b == 0 else flip(x, axis, b) for b in range(0, lax.axis_size(axis), step)}


def gather_tensor(x):
    me = lax.axis_index("tensor")
    held = gather_far(x, "tensor", 2)
    whole = jnp.zeros((x.shape[0] * lax.axis_size("tensor"),) + x.shape[1:], x.dtype)
    for b, block in held.items():
        whole = put(whole, block, me ^ b)
        whole = put(whole, flip(block, "tensor", 1), me ^ b ^ 1)
    return whole


def gather_dp(x):
    me = lax.axis_index("dp")
    whole = jnp.zeros((x.shape[0] * lax.axis_size("dp"),) + x.shape[1:], x.dtype)
    for b, block in gather_far(x, "dp", 1).items():
        whole = put(whole, block, me ^ b)
    return whole


def scatter_dp(x):
    n = lax.axis_size("dp")
    me = lax.axis_index("dp")
    count = x.shape[0] // n
    got = [flip(rows(x, me ^ b, count), "dp", b) for b in range(n - 1, 0, -1)]
    total = rows(x, me, count).astype(jnp.float32)
    for piece in got:
        total = total + piece.astype(jnp.float32)
    return total


def scatter_tensor(x):
    n = lax.axis_size("tensor")
    me = lax.axis_index("tensor")
    count = x.shape[0] // n
    total = None
    for b in range(n - 2, -1, -2):
        mate = flip(rows(x, me ^ b ^ 1, count), "tensor", 1).astype(jnp.float32)
        pair = rows(x, me ^ b, count).astype(jnp.float32) + mate
        if b:
            pair = flip(pair.astype(x.dtype), "tensor", b).astype(jnp.float32)
        total = pair if total is None else total + pair
    return total


def sum_all(x, axis):
    bits = 1
    while bits < lax.axis_size(axis):
        x = x + flip(x, axis, bits)
        bits *= 2
    return x


def shards(
    tokens,
    cotangent,
    gate_weight,
    up_weight,
    down_weight,
    gate_in,
    up_in,
    down_out,
    gate_out,
    up_out,
    down_in,
    tenants,
    owners,
):
    highest = lax.Precision.HIGHEST
    dp_count = lax.axis_size("dp")
    tensor_count = lax.axis_size("tensor")
    dp_index = lax.axis_index("dp")
    tensor_index = lax.axis_index("tensor")
    rows_in, feat_here = tokens.shape
    width_here = gate_weight.shape[1]
    rank = gate_in.shape[2]
    token_count = rows_in * tensor_count
    group_rows = token_count // dp_count
    blocks_all = tenants.shape[0]
    blocks_group = group_rows // BLOCK
    blocks_in = rows_in // BLOCK
    tenant_count = owners.shape[0]
    slots_here = tenant_count // dp_count
    tenants_here = tenant_count // tensor_count
    columns = tenant_count * rank
    bf16 = jnp.bfloat16

    def pick(table, index):
        at = jnp.arange(table.shape[0], dtype=jnp.int32)
        return jnp.sum(jnp.where(index[:, None] == at[None, :], table[None, :], 0), axis=1)

    def mask_of(block_values, first, count):
        n = block_values.shape[0]
        column = lax.broadcasted_iota(jnp.int32, (n, BLOCK, count * rank), 2) // rank + first
        return (block_values[:, None, None] == column).reshape(n * BLOCK, count * rank)

    def tile(count):
        r = lax.broadcasted_iota(jnp.int32, (rank, count * rank), 0)
        c = lax.broadcasted_iota(jnp.int32, (rank, count * rank), 1)
        return (c % rank == r).astype(bf16)

    def expand(r, mask):
        wide = dot(r, tile(mask.shape[1] // rank))
        return jnp.where(mask, wide, 0.0).astype(bf16)

    def collapse(wide, mask):
        narrow = jnp.where(mask, wide, jnp.zeros_like(wide))
        t = tile(mask.shape[1] // rank).astype(wide.dtype)
        return dot(narrow, t, 1, 1, highest if wide.dtype == jnp.float32 else None)

    def as_rows(table):
        return table.transpose(0, 2, 1).reshape(columns, table.shape[1])

    arange = lambda n: jnp.arange(n, dtype=jnp.int32)
    group_tenants = pick(tenants, dp_index * blocks_group + arange(blocks_group))
    input_tenants = pick(tenants, tensor_index * blocks_in + arange(blocks_in))
    block_slots = pick(owners, tenants)
    mask_all = mask_of(tenants, 0, tenant_count)
    mask_group = mask_of(group_tenants, 0, tenant_count)
    mask_input = mask_of(input_tenants, 0, tenant_count)
    mask_held = mask_of(tenants, tensor_index * tenants_here, tenants_here)
    mask_slots = mask_of(block_slots, dp_index * slots_here, slots_here)
    mask_local = mask_of(arange(blocks_group), 0, blocks_group)
    gate_raise = gate_out.reshape(columns, width_here)
    up_raise = up_out.reshape(columns, width_here)
    down_raise = down_out.reshape(columns, feat_here)

    all_inputs = gather_tensor(tokens)
    all_cot = gather_tensor(cotangent)

    gate_sum = scatter_dp(dot(all_inputs, gate_weight).astype(bf16))
    rank_parts = jnp.concatenate(
        [
            collapse(dot(all_inputs, as_rows(table), 1, 1).astype(bf16), mask_all)
            for table in (gate_in, up_in)
        ],
        axis=1,
    ).astype(bf16)
    ranks = scatter_dp(rank_parts).astype(bf16)
    gate_rank, up_rank = ranks[:, :rank], ranks[:, rank:]
    up_sum = scatter_dp(dot(all_inputs, up_weight).astype(bf16))

    gate_full = gate_sum + adapter_scale * dot(expand(gate_rank, mask_group), gate_raise)
    up_full = up_sum + adapter_scale * dot(expand(up_rank, mask_group), up_raise)
    hidden = (jax.nn.silu(gate_full) * up_full).astype(bf16)
    all_hidden = gather_dp(hidden)

    down_back = adapter_scale * collapse(dot(all_cot, down_raise, 1, 1), mask_all)
    down_back = sum_all(down_back, "dp").astype(bf16)
    group_down_back = rows(down_back, dp_index, group_rows)
    down_drop = as_rows(down_in)
    hidden_grad = scatter_dp(dot(all_cot, down_weight, 1, 1).astype(bf16))
    hidden_grad = hidden_grad + dot(expand(group_down_back, mask_group), down_drop)

    out_sum = scatter_tensor(dot(all_hidden, down_weight).astype(bf16))
    down_rank = collapse(dot(all_hidden, down_drop, 1, 1).astype(bf16), mask_all)
    down_rank = sum_all(down_rank, "tensor").astype(bf16)
    own_down_rank = rows(down_rank, tensor_index, rows_in)
    mixed = (
        out_sum + adapter_scale * dot(expand(own_down_rank, mask_input), down_raise)
    ).astype(bf16)
    grad_down_out = adapter_scale * dot(expand(down_rank, mask_held), all_cot, 0, 0)
    grad_down_out = grad_down_out.reshape(tenants_here, rank, feat_here)

    sig = jax.nn.sigmoid(gate_full)
    up_grad = (hidden_grad * gate_full * sig).astype(bf16)
    gate_grad = (hidden_grad * up_full * sig * (1.0 + gate_full * (1.0 - sig))).astype(bf16)
    backs = adapter_scale * jnp.concatenate(
        [
            collapse(dot(gate_grad, gate_raise, 1, 1), mask_group),
            collapse(dot(up_grad, up_raise, 1, 1), mask_group),
        ],
        axis=1,
    )
    backs = gather_dp(sum_all(backs, "tensor").astype(bf16))

    lifts = adapter_scale * jnp.concatenate(
        [
            dot(expand(gate_rank, mask_local), gate_grad, 0, 0),
            dot(expand(up_rank, mask_local), up_grad, 0, 0),
        ],
        axis=0,
    )
    lifts = gather_dp(lifts.astype(bf16))

    def own_lift(which):
        shape = (slots_here, rank, dp_count, 2, blocks_group, rank)
        iota = lambda axis: lax.broadcasted_iota(jnp.int32, shape, axis)
        slots = block_slots.reshape(1, 1, dp_count, 1, blocks_group, 1)
        chosen = (
            (iota(0) + dp_index * slots_here == slots) & (iota(1) == iota(5)) & (iota(3) == which)
        )
        chosen = chosen.astype(bf16).reshape(slots_here * rank, lifts.shape[0])
        return dot(chosen, lifts).reshape(slots_here, rank, width_here)

    grad_gate_out = own_lift(0)
    grad_up_out = own_lift(1)

    def own_in(back, mask, source, count):
        grad = dot(expand(back, mask), source, 0, 0)
        return grad.reshape(count, rank, source.shape[1]).transpose(0, 2, 1)

    grad_gate_in = own_in(backs[:, :rank], mask_held, all_inputs, tenants_here)
    grad_up_in = own_in(backs[:, rank:], mask_held, all_inputs, tenants_here)
    grad_down_in = own_in(down_back, mask_slots, all_hidden, slots_here)
    return (
        mixed,
        grad_gate_in,
        grad_up_in,
        grad_down_out,
        grad_gate_out,
        grad_up_out,
        grad_down_in,
    )


def solution(mesh):
    in_specs = (
        P("tensor", "dp"),
        P("tensor", "dp"),
        P("dp", "tensor"),
        P("dp", "tensor"),
        P("tensor", "dp"),
        P(None, "dp", None),
        P(None, "dp", None),
        P(None, None, "dp"),
        P(None, None, "tensor"),
        P(None, None, "tensor"),
        P(None, "tensor", None),
        P(),
        P(),
    )
    out_specs = (
        P("tensor", "dp"),
        P("tensor", "dp", None),
        P("tensor", "dp", None),
        P("tensor", None, "dp"),
        P("dp", None, "tensor"),
        P("dp", None, "tensor"),
        P("dp", "tensor", None),
    )
    return jax.shard_map(shards, mesh=mesh, in_specs=in_specs, out_specs=out_specs, check_vma=False)
```

```python
import jax
import jax.numpy as jnp
from jax import lax
from jax.sharding import PartitionSpec as P

BLOCK = 64


adapter_scale = 0.5


def dot(a, b, ca=1, cb=0, precision=None):
    return lax.dot_general(
        a,
        b,
        (((ca,), (cb,)), ((), ())),
        preferred_element_type=jnp.float32,
        precision=precision,
    )


def flip(x, axis, bits):
    n = lax.axis_size(axis)
    return lax.ppermute(x, axis, [(i, i ^ bits) for i in range(n)])


def rows(x, index, count):
    return lax.dynamic_slice_in_dim(x, index * count, count)


def after(x, *done):
    return lax.optimization_barrier((x,) + done)[0]


def reorder(x, axis):
    n = lax.axis_size(axis)
    me = lax.axis_index(axis)
    bits = 1
    while bits < n:
        half = x.shape[0] // n * bits
        pieces = [x[i * half : (i + 1) * half] for i in range(n // bits)]
        swapped = jnp.concatenate([pieces[i ^ 1] for i in range(n // bits)])
        x = jnp.where((me // bits) % 2 == 1, swapped, x)
        bits *= 2
    return x


def far_blocks(x, axis, step):
    return [x if b == 0 else flip(x, axis, b) for b in range(0, lax.axis_size(axis), step)]


def with_mates(far):
    return jnp.concatenate([block for own in far for block in (own, flip(own, "tensor", 1))])


def scatter_dp(x):
    n = lax.axis_size("dp")
    me = lax.axis_index("dp")
    mine = lax.axis_index("tensor")
    size = lax.axis_size("tensor")
    per = size // n
    count = x.shape[0] // size

    def group(g):
        return jnp.concatenate([rows(x, (g * per + i) ^ mine, count) for i in range(per)])

    got = [flip(group(me ^ b), "dp", b) for b in range(n - 1, 0, -1)]
    total = group(me).astype(jnp.float32)
    for piece in got:
        total = total + piece.astype(jnp.float32)
    return total


def scatter_tensor(x):
    n = lax.axis_size("tensor")
    me = lax.axis_index("tensor")
    per = n // lax.axis_size("dp")
    other = lax.axis_index("dp")
    count = x.shape[0] // n

    def block(a):
        return rows(x, ((a // per) ^ other) * per + a % per, count)

    total = None
    for b in range(n - 2, -1, -2):
        mate = flip(block(me ^ b ^ 1), "tensor", 1).astype(jnp.float32)
        pair = block(me ^ b).astype(jnp.float32) + mate
        if b:
            pair = flip(pair.astype(x.dtype), "tensor", b).astype(jnp.float32)
        total = pair if total is None else total + pair
    return total


def sum_all(x, axis):
    bits = 1
    while bits < lax.axis_size(axis):
        x = x + flip(x, axis, bits)
        bits *= 2
    return x


def shards(
    tokens,
    cotangent,
    gate_weight,
    up_weight,
    down_weight,
    gate_in,
    up_in,
    down_out,
    gate_out,
    up_out,
    down_in,
    tenants,
    owners,
):
    highest = lax.Precision.HIGHEST
    dp_count = lax.axis_size("dp")
    tensor_count = lax.axis_size("tensor")
    dp_index = lax.axis_index("dp")
    tensor_index = lax.axis_index("tensor")
    rows_in, feat_here = tokens.shape
    width_here = gate_weight.shape[1]
    rank = gate_in.shape[2]
    token_count = rows_in * tensor_count
    group_rows = token_count // dp_count
    blocks_all = tenants.shape[0]
    blocks_group = group_rows // BLOCK
    blocks_in = rows_in // BLOCK
    tenant_count = owners.shape[0]
    slots_here = tenant_count // dp_count
    tenants_here = tenant_count // tensor_count
    columns = tenant_count * rank
    bf16 = jnp.bfloat16

    def pick(table, index):
        at = jnp.arange(table.shape[0], dtype=jnp.int32)
        return jnp.sum(jnp.where(index[:, None] == at[None, :], table[None, :], 0), axis=1)

    def mask_of(block_values, first, count):
        n = block_values.shape[0]
        column = lax.broadcasted_iota(jnp.int32, (n, BLOCK, count * rank), 2) // rank + first
        return (block_values[:, None, None] == column).reshape(n * BLOCK, count * rank)

    def tile(count):
        r = lax.broadcasted_iota(jnp.int32, (rank, count * rank), 0)
        c = lax.broadcasted_iota(jnp.int32, (rank, count * rank), 1)
        return (c % rank == r).astype(bf16)

    def expand(r, mask):
        wide = dot(r, tile(mask.shape[1] // rank))
        return jnp.where(mask, wide, 0.0).astype(bf16)

    def collapse(wide, mask):
        narrow = jnp.where(mask, wide, jnp.zeros_like(wide))
        t = tile(mask.shape[1] // rank).astype(wide.dtype)
        return dot(narrow, t, 1, 1, highest if wide.dtype == jnp.float32 else None)

    def as_rows(table):
        return table.transpose(0, 2, 1).reshape(columns, table.shape[1])

    arange = lambda n: jnp.arange(n, dtype=jnp.int32)
    group_tenants = pick(tenants, dp_index * blocks_group + arange(blocks_group))
    input_tenants = pick(tenants, tensor_index * blocks_in + arange(blocks_in))
    block_slots = pick(owners, tenants)
    near = arange(blocks_all)
    near = ((near // blocks_in) ^ tensor_index) * blocks_in + near % blocks_in
    across = arange(blocks_all)
    across = ((across // blocks_group) ^ dp_index) * blocks_group + across % blocks_group
    near_tenants = pick(tenants, near)
    across_tenants = pick(tenants, across)
    across_slots = pick(block_slots, across)
    mask_near = mask_of(near_tenants, 0, tenant_count)
    mask_across = mask_of(across_tenants, 0, tenant_count)
    mask_group = mask_of(group_tenants, 0, tenant_count)
    mask_input = mask_of(input_tenants, 0, tenant_count)
    mask_held = mask_of(near_tenants, tensor_index * tenants_here, tenants_here)
    mask_slots = mask_of(across_slots, dp_index * slots_here, slots_here)
    mask_local = mask_of(arange(blocks_group), 0, blocks_group)
    gate_raise = gate_out.reshape(columns, width_here)
    up_raise = up_out.reshape(columns, width_here)
    down_raise = down_out.reshape(columns, feat_here)

    far_tokens = far_blocks(tokens, "tensor", 2)
    all_inputs = with_mates(far_tokens)
    far_cot = far_blocks(after(cotangent, *far_tokens), "tensor", 2)
    all_cot = with_mates(far_cot)

    gate_sum = scatter_dp(dot(all_inputs, gate_weight).astype(bf16))
    rank_parts = jnp.concatenate(
        [
            collapse(dot(all_inputs, as_rows(table), 1, 1).astype(bf16), mask_near)
            for table in (gate_in, up_in)
        ],
        axis=1,
    ).astype(bf16)
    ranks = scatter_dp(rank_parts).astype(bf16)
    gate_rank, up_rank = ranks[:, :rank], ranks[:, rank:]
    up_sum = scatter_dp(dot(all_inputs, up_weight).astype(bf16))

    gate_full = gate_sum + adapter_scale * dot(expand(gate_rank, mask_group), gate_raise)
    up_full = up_sum + adapter_scale * dot(expand(up_rank, mask_group), up_raise)
    hidden = (jax.nn.silu(gate_full) * up_full).astype(bf16)
    far_hidden = far_blocks(hidden, "dp", 1)
    all_hidden = jnp.concatenate(far_hidden)

    down_back = adapter_scale * collapse(dot(all_cot, down_raise, 1, 1), mask_near)
    down_back = reorder(sum_all(down_back, "dp"), "tensor").astype(bf16)
    group_down_back = rows(down_back, dp_index, group_rows)
    down_drop = as_rows(down_in)
    hidden_grad_part = dot(all_cot, down_weight, 1, 1).astype(bf16)
    hidden_grad = scatter_dp(after(hidden_grad_part, *far_hidden))
    hidden_grad = hidden_grad + dot(expand(group_down_back, mask_group), down_drop)

    out_part = dot(all_hidden, down_weight).astype(bf16)
    out_sum = scatter_tensor(out_part)
    hidden_grad = after(hidden_grad, out_part)
    down_rank = collapse(dot(all_hidden, down_drop, 1, 1).astype(bf16), mask_across)
    down_rank = reorder(sum_all(down_rank, "tensor"), "dp").astype(bf16)
    own_down_rank = rows(down_rank, tensor_index, rows_in)
    mixed = (
        out_sum + adapter_scale * dot(expand(own_down_rank, mask_input), down_raise)
    ).astype(bf16)
    grad_down_out = adapter_scale * dot(
        expand(reorder(down_rank, "tensor"), mask_held), all_cot, 0, 0
    )
    grad_down_out = grad_down_out.reshape(tenants_here, rank, feat_here)

    sig = jax.nn.sigmoid(gate_full)
    up_grad = (hidden_grad * gate_full * sig).astype(bf16)
    gate_grad = (hidden_grad * up_full * sig * (1.0 + gate_full * (1.0 - sig))).astype(bf16)
    backs = adapter_scale * jnp.concatenate(
        [
            collapse(dot(gate_grad, gate_raise, 1, 1), mask_group),
            collapse(dot(up_grad, up_raise, 1, 1), mask_group),
        ],
        axis=1,
    )
    backs = sum_all(backs, "tensor").astype(bf16)
    backs = jnp.concatenate(far_blocks(backs, "dp", 1))
    backs = reorder(reorder(backs, "dp"), "tensor")

    lifts = adapter_scale * jnp.concatenate(
        [
            dot(expand(gate_rank, mask_local), gate_grad, 0, 0),
            dot(expand(up_rank, mask_local), up_grad, 0, 0),
        ],
        axis=0,
    )
    lifts = jnp.concatenate(far_blocks(lifts.astype(bf16), "dp", 1))

    def own_lift(which):
        shape = (slots_here, rank, dp_count, 2, blocks_group, rank)
        iota = lambda axis: lax.broadcasted_iota(jnp.int32, shape, axis)
        slots = across_slots.reshape(1, 1, dp_count, 1, blocks_group, 1)
        chosen = (
            (iota(0) + dp_index * slots_here == slots) & (iota(1) == iota(5)) & (iota(3) == which)
        )
        chosen = chosen.astype(bf16).reshape(slots_here * rank, lifts.shape[0])
        return dot(chosen, lifts).reshape(slots_here, rank, width_here)

    grad_gate_out = own_lift(0)
    grad_up_out = own_lift(1)

    def own_in(back, mask, source, count):
        grad = dot(expand(back, mask), source, 0, 0)
        return grad.reshape(count, rank, source.shape[1]).transpose(0, 2, 1)

    grad_gate_in = own_in(backs[:, :rank], mask_held, all_inputs, tenants_here)
    grad_up_in = own_in(backs[:, rank:], mask_held, all_inputs, tenants_here)
    grad_down_in = own_in(reorder(down_back, "dp"), mask_slots, all_hidden, slots_here)
    return (
        mixed,
        grad_gate_in,
        grad_up_in,
        grad_down_out,
        grad_gate_out,
        grad_up_out,
        grad_down_in,
    )


def solution(mesh):
    in_specs = (
        P("tensor", "dp"),
        P("tensor", "dp"),
        P("dp", "tensor"),
        P("dp", "tensor"),
        P("tensor", "dp"),
        P(None, "dp", None),
        P(None, "dp", None),
        P(None, None, "dp"),
        P(None, None, "tensor"),
        P(None, None, "tensor"),
        P(None, "tensor", None),
        P(),
        P(),
    )
    out_specs = (
        P("tensor", "dp"),
        P("tensor", "dp", None),
        P("tensor", "dp", None),
        P("tensor", None, "dp"),
        P("dp", None, "tensor"),
        P("dp", None, "tensor"),
        P("dp", "tensor", None),
    )
    return jax.shard_map(shards, mesh=mesh, in_specs=in_specs, out_specs=out_specs, check_vma=False)
```

```python
import jax
import jax.numpy as jnp
from jax import lax
from jax.sharding import PartitionSpec as P

BLOCK = 64


adapter_scale = 0.5


def dot(a, b, ca=1, cb=0, precision=None):
    return lax.dot_general(
        a,
        b,
        (((ca,), (cb,)), ((), ())),
        preferred_element_type=jnp.float32,
        precision=precision,
    )


def flip(x, axis, bits):
    n = lax.axis_size(axis)
    return lax.ppermute(x, axis, [(i, i ^ bits) for i in range(n)])


def rows(x, index, count):
    return lax.dynamic_slice_in_dim(x, index * count, count)


def after(x, *done):
    return lax.optimization_barrier((x,) + done)[0]


def reorder(x, axis):
    n = lax.axis_size(axis)
    me = lax.axis_index(axis)
    bits = 1
    while bits < n:
        half = x.shape[0] // n * bits
        pieces = [x[i * half : (i + 1) * half] for i in range(n // bits)]
        swapped = jnp.concatenate([pieces[i ^ 1] for i in range(n // bits)])
        x = jnp.where((me // bits) % 2 == 1, swapped, x)
        bits *= 2
    return x


def far_blocks(x, axis, step):
    return [x if b == 0 else flip(x, axis, b) for b in range(0, lax.axis_size(axis), step)]


def with_mates(far):
    return jnp.concatenate([block for own in far for block in (own, flip(own, "tensor", 1))])


def with_mates_at_once(far):
    count = far[0].shape[0]
    mates = flip(jnp.concatenate(far), "tensor", 1)
    pieces = []
    for i, own in enumerate(far):
        pieces += [own, mates[i * count : (i + 1) * count]]
    return jnp.concatenate(pieces)


def scatter_dp(*parts):
    n = lax.axis_size("dp")
    me = lax.axis_index("dp")
    mine = lax.axis_index("tensor")
    size = lax.axis_size("tensor")
    per = size // n
    count = parts[0].shape[0] // size

    def group(g):
        return jnp.concatenate(
            [
                jnp.concatenate([rows(x, (g * per + i) ^ mine, count) for i in range(per)])
                for x in parts
            ],
            axis=1,
        )

    got = [flip(group(me ^ b), "dp", b) for b in range(n - 1, 0, -1)]
    total = group(me).astype(jnp.float32)
    for piece in got:
        total = total + piece.astype(jnp.float32)
    return total


def scatter_tensor(x):
    n = lax.axis_size("tensor")
    me = lax.axis_index("tensor")
    per = n // lax.axis_size("dp")
    other = lax.axis_index("dp")
    count = x.shape[0] // n

    def block(a):
        return rows(x, ((a // per) ^ other) * per + a % per, count)

    total = None
    far = range(n - 2, -1, -2)
    mates = flip(jnp.concatenate([block(me ^ b ^ 1) for b in far]), "tensor", 1)
    for i, b in enumerate(far):
        mate = mates[i * count : (i + 1) * count].astype(jnp.float32)
        pair = block(me ^ b).astype(jnp.float32) + mate
        if b:
            pair = flip(pair.astype(x.dtype), "tensor", b).astype(jnp.float32)
        total = pair if total is None else total + pair
    return total


def sum_all(x, axis):
    bits = 1
    while bits < lax.axis_size(axis):
        x = x + flip(x, axis, bits)
        bits *= 2
    return x


def shards(
    tokens,
    cotangent,
    gate_weight,
    up_weight,
    down_weight,
    gate_in,
    up_in,
    down_out,
    gate_out,
    up_out,
    down_in,
    tenants,
    owners,
):
    highest = lax.Precision.HIGHEST
    dp_count = lax.axis_size("dp")
    tensor_count = lax.axis_size("tensor")
    dp_index = lax.axis_index("dp")
    tensor_index = lax.axis_index("tensor")
    rows_in, feat_here = tokens.shape
    width_here = gate_weight.shape[1]
    rank = gate_in.shape[2]
    token_count = rows_in * tensor_count
    group_rows = token_count // dp_count
    blocks_all = tenants.shape[0]
    blocks_group = group_rows // BLOCK
    blocks_in = rows_in // BLOCK
    tenant_count = owners.shape[0]
    slots_here = tenant_count // dp_count
    tenants_here = tenant_count // tensor_count
    columns = tenant_count * rank
    bf16 = jnp.bfloat16

    def pick(table, index):
        at = jnp.arange(table.shape[0], dtype=jnp.int32)
        return jnp.sum(jnp.where(index[:, None] == at[None, :], table[None, :], 0), axis=1)

    def mask_of(block_values, first, count):
        n = block_values.shape[0]
        column = lax.broadcasted_iota(jnp.int32, (n, BLOCK, count * rank), 2) // rank + first
        return (block_values[:, None, None] == column).reshape(n * BLOCK, count * rank)

    def tile(count):
        r = lax.broadcasted_iota(jnp.int32, (rank, count * rank), 0)
        c = lax.broadcasted_iota(jnp.int32, (rank, count * rank), 1)
        return (c % rank == r).astype(bf16)

    def expand(r, mask):
        wide = dot(r, tile(mask.shape[1] // rank))
        return jnp.where(mask, wide, 0.0).astype(bf16)

    def collapse(wide, mask):
        narrow = jnp.where(mask, wide, jnp.zeros_like(wide))
        t = tile(mask.shape[1] // rank).astype(wide.dtype)
        return dot(narrow, t, 1, 1, highest if wide.dtype == jnp.float32 else None)

    def as_rows(table):
        return table.transpose(0, 2, 1).reshape(columns, table.shape[1])

    arange = lambda n: jnp.arange(n, dtype=jnp.int32)
    group_tenants = pick(tenants, dp_index * blocks_group + arange(blocks_group))
    input_tenants = pick(tenants, tensor_index * blocks_in + arange(blocks_in))
    block_slots = pick(owners, tenants)
    near = arange(blocks_all)
    near = ((near // blocks_in) ^ tensor_index) * blocks_in + near % blocks_in
    across = arange(blocks_all)
    across = ((across // blocks_group) ^ dp_index) * blocks_group + across % blocks_group
    near_tenants = pick(tenants, near)
    across_tenants = pick(tenants, across)
    across_slots = pick(block_slots, across)
    mask_near = mask_of(near_tenants, 0, tenant_count)
    mask_across = mask_of(across_tenants, 0, tenant_count)
    mask_group = mask_of(group_tenants, 0, tenant_count)
    mask_input = mask_of(input_tenants, 0, tenant_count)
    mask_held = mask_of(near_tenants, tensor_index * tenants_here, tenants_here)
    mask_slots = mask_of(across_slots, dp_index * slots_here, slots_here)
    mask_local = mask_of(arange(blocks_group), 0, blocks_group)
    gate_raise = gate_out.reshape(columns, width_here)
    up_raise = up_out.reshape(columns, width_here)
    down_raise = down_out.reshape(columns, feat_here)

    far_tokens = far_blocks(tokens, "tensor", 2)
    all_inputs = with_mates(far_tokens)
    far_cot = far_blocks(after(cotangent, *far_tokens), "tensor", 2)
    all_cot = with_mates_at_once(far_cot)

    gate_sum = scatter_dp(dot(all_inputs, gate_weight).astype(bf16))
    rank_parts = jnp.concatenate(
        [
            collapse(dot(all_inputs, as_rows(table), 1, 1).astype(bf16), mask_near)
            for table in (gate_in, up_in)
        ],
        axis=1,
    ).astype(bf16)
    up_sums = scatter_dp(dot(all_inputs, up_weight).astype(bf16), rank_parts)
    up_sum = up_sums[:, :width_here]
    gate_rank = up_sums[:, width_here : width_here + rank].astype(bf16)
    up_rank = up_sums[:, width_here + rank :].astype(bf16)

    gate_full = gate_sum + adapter_scale * dot(expand(gate_rank, mask_group), gate_raise)
    up_full = up_sum + adapter_scale * dot(expand(up_rank, mask_group), up_raise)
    hidden = (jax.nn.silu(gate_full) * up_full).astype(bf16)
    far_hidden = far_blocks(hidden, "dp", 1)
    all_hidden = jnp.concatenate(far_hidden)

    down_back = adapter_scale * collapse(dot(all_cot, down_raise, 1, 1), mask_near)
    down_back = after(down_back, *far_hidden)
    down_back = reorder(sum_all(down_back, "dp"), "tensor").astype(bf16)
    group_down_back = rows(down_back, dp_index, group_rows)
    down_drop = as_rows(down_in)
    hidden_grad_part = dot(all_cot, down_weight, 1, 1).astype(bf16)
    hidden_grad = scatter_dp(after(hidden_grad_part, *far_hidden))
    hidden_grad = hidden_grad + dot(expand(group_down_back, mask_group), down_drop)

    out_part = dot(all_hidden, down_weight).astype(bf16)
    out_sum = scatter_tensor(out_part)
    hidden_grad = after(hidden_grad, out_part)
    down_rank = collapse(dot(all_hidden, down_drop, 1, 1).astype(bf16), mask_across)
    down_rank = reorder(sum_all(down_rank, "tensor"), "dp").astype(bf16)
    own_down_rank = rows(down_rank, tensor_index, rows_in)
    mixed = (
        out_sum + adapter_scale * dot(expand(own_down_rank, mask_input), down_raise)
    ).astype(bf16)
    grad_down_out = adapter_scale * dot(
        expand(reorder(down_rank, "tensor"), mask_held), all_cot, 0, 0
    )
    grad_down_out = grad_down_out.reshape(tenants_here, rank, feat_here)

    sig = jax.nn.sigmoid(gate_full)
    up_grad = (hidden_grad * gate_full * sig).astype(bf16)
    gate_grad = (hidden_grad * up_full * sig * (1.0 + gate_full * (1.0 - sig))).astype(bf16)
    backs = adapter_scale * jnp.concatenate(
        [
            collapse(dot(gate_grad, gate_raise, 1, 1), mask_group),
            collapse(dot(up_grad, up_raise, 1, 1), mask_group),
        ],
        axis=1,
    )
    backs = sum_all(backs, "tensor").astype(bf16)
    backs = jnp.concatenate(far_blocks(backs, "dp", 1))
    backs = reorder(reorder(backs, "dp"), "tensor")

    lifts = adapter_scale * jnp.concatenate(
        [
            dot(expand(gate_rank, mask_local), gate_grad, 0, 0),
            dot(expand(up_rank, mask_local), up_grad, 0, 0),
        ],
        axis=0,
    )
    lifts = jnp.concatenate(far_blocks(lifts.astype(bf16), "dp", 1))

    def own_lift(which):
        shape = (slots_here, rank, dp_count, 2, blocks_group, rank)
        iota = lambda axis: lax.broadcasted_iota(jnp.int32, shape, axis)
        slots = across_slots.reshape(1, 1, dp_count, 1, blocks_group, 1)
        chosen = (
            (iota(0) + dp_index * slots_here == slots) & (iota(1) == iota(5)) & (iota(3) == which)
        )
        chosen = chosen.astype(bf16).reshape(slots_here * rank, lifts.shape[0])
        return dot(chosen, lifts).reshape(slots_here, rank, width_here)

    grad_gate_out = own_lift(0)
    grad_up_out = own_lift(1)

    def own_in(back, mask, source, count):
        grad = dot(expand(back, mask), source, 0, 0)
        return grad.reshape(count, rank, source.shape[1]).transpose(0, 2, 1)

    grad_gate_in = own_in(backs[:, :rank], mask_held, all_inputs, tenants_here)
    grad_up_in = own_in(backs[:, rank:], mask_held, all_inputs, tenants_here)
    grad_down_in = own_in(reorder(down_back, "dp"), mask_slots, all_hidden, slots_here)
    return (
        mixed,
        grad_gate_in,
        grad_up_in,
        grad_down_out,
        grad_gate_out,
        grad_up_out,
        grad_down_in,
    )


def solution(mesh):
    in_specs = (
        P("tensor", "dp"),
        P("tensor", "dp"),
        P("dp", "tensor"),
        P("dp", "tensor"),
        P("tensor", "dp"),
        P(None, "dp", None),
        P(None, "dp", None),
        P(None, None, "dp"),
        P(None, None, "tensor"),
        P(None, None, "tensor"),
        P(None, "tensor", None),
        P(),
        P(),
    )
    out_specs = (
        P("tensor", "dp"),
        P("tensor", "dp", None),
        P("tensor", "dp", None),
        P("tensor", None, "dp"),
        P("dp", None, "tensor"),
        P("dp", None, "tensor"),
        P("dp", "tensor", None),
    )
    return jax.shard_map(shards, mesh=mesh, in_specs=in_specs, out_specs=out_specs, check_vma=False)
```
